32 devices in a mesh: groups: 2 (over y), shard: 4 (over z), sub: 2 (over x), cores: 2 (over core).
Axes of the slice: x: 2, y: 2, z: 4, core: 2. Of those that a mesh axis runs over, the one named last changes fastest.
Arguments:
- embeddings: float32 [32768, 768], P(('groups', 'shard', 'sub', 'cores')), parts along dimension 0, may hold values from -30 to 30
- bucket_pos: int32 [32768], P(('groups', 'shard', 'sub', 'cores')), parts along dimension 0, may hold values from 0 to 16383, as said below
- tile_valid: int32 [8, 4], P(('groups', 'sub', 'cores')), parts along dimension 0, may hold values from 512 to 1024, as said below
- pair_mask: int32 [8, 4], P(('groups', 'sub', 'cores')), parts along dimension 0, may hold values 0 or 1
Outputs:
- neighbour_sums: float32 [8, 4096, 768], P(('groups', 'sub', 'cores'), 'shard'), parts along dimension 0
The draws below stay inside these ranges and needn't reach their ends.
There are 2 independent parts, one for each index of `groups`. The reference program is written for one: setup_inputs(seed, part) draws one part's arguments, and reference() takes and returns one part's arrays. A program takes and returns all parts, laid end to end along the dimension named above; each array names one. Nothing has to cross between parts.
Inputs may be any that keep to these rules, and one draw needn't show every extreme that they name: `bucket_pos`: A permutation giving every ingest row its own place in bucket order. Of the 1024 rows of one ingest block (one device's rows), at most 128 go to any one tile, and every block sends exactly 128 rows to some tile. `tile_valid`: rows of a tile past its count are padding.
All inputs are finite; a program needn't handle non-finite values. No bound on the sum of `pair_mask` on one device may be relied on, other than what follows from the above.
Results may differ from the reference program's by a relative error of at most 0.0023.
Values may be sent and summed in bfloat16 or wider, within the bound.
A program may use at most 64 MiB of HBM per device.

```python
import math
import jax
import jax.numpy as jnp
from jax import lax

D = 768
TILE = 1024
BANDS = 4
OWNERS = 16
BAND_ROWS = 4096
DOCS = 16384
N_SHARD = 4


def bucket_layout(key):
    key = jax.random.fold_in(key, 5)
    key_shift, key_owner, key_order = jax.random.split(key, 3)
    mean_rows = TILE // OWNERS
    spin = jax.random.permutation(key_shift, OWNERS)
    excess = jnp.where(spin < OWNERS // 4, mean_rows, jnp.where(spin < OWNERS // 2, -mean_rows, 0))
    source = jnp.arange(OWNERS)[:, None]
    target = jnp.arange(OWNERS)[None, :]
    counts = mean_rows + excess[(target - source) % OWNERS]
    ends = jnp.cumsum(counts, axis=1)
    starts = ends - counts
    before = jnp.cumsum(counts, axis=0) - counts
    slots = jnp.arange(TILE)

    def find_owner(row_ends):
        return jnp.searchsorted(row_ends, slots, side='right')
    dest = jax.vmap(find_owner)(ends)
    rank_in = slots[None, :] - jnp.take_along_axis(starts, dest, axis=1)
    local = jnp.take_along_axis(before, dest, axis=1) + rank_in

    def shuffle(sub_key):
        return jax.random.permutation(sub_key, TILE)
    shuffles = jax.vmap(shuffle)(jax.random.split(key_owner, OWNERS))
    local = shuffles[dest, local]
    position = dest % BANDS * BAND_ROWS + dest // BANDS * TILE + local
    orders = jax.vmap(shuffle)(jax.random.split(key_order, OWNERS))
    position = jnp.take_along_axis(position, orders, axis=1)
    return position.reshape(DOCS).astype(jnp.int32)


def draw_bucket_pos(key, part):
    return bucket_layout(key)


def draw_embeddings(key, part):
    position = bucket_layout(key)
    key = jax.random.fold_in(key, 11)
    keys = jax.random.split(key, 5)
    jitter = jax.random.randint(keys[0], (DOCS,), 0, TILE)
    cluster = (jnp.arange(DOCS) + jitter) // 8
    centres = jnp.clip(jax.random.normal(keys[1], (DOCS // 8 + TILE // 8 + 1, D), jnp.float32), -3.5, 3.5)
    noise = jnp.clip(jax.random.normal(keys[2], (DOCS, D), jnp.float32), -3.5, 3.5)
    column = jnp.exp(jax.random.uniform(keys[3], (D,), jnp.float32, math.log(0.5), math.log(2.0)))
    row_scale = jnp.exp(jax.random.uniform(keys[4], (DOCS,), jnp.float32, math.log(0.3), math.log(3.0)))
    in_bucket = row_scale[:, None] * column[None, :] * (0.9 * centres[cluster] + 0.44 * noise)
    return in_bucket[position]


def draw_tile_valid(key, part):
    key = jax.random.fold_in(key, 7)
    key_count, key_full = jax.random.split(key, 2)
    counts = jax.random.randint(key_count, (BANDS * N_SHARD,), TILE // 2, TILE + 1)
    full_at = jax.random.randint(key_full, (), 0, BANDS * N_SHARD)
    counts = counts.at[full_at].set(TILE)
    return counts.reshape(BANDS, N_SHARD).astype(jnp.int32)


def place_ends(drawn, stream_key, smallest, high):
    spot = [jax.random.randint(jax.random.fold_in(stream_key, axis), (), 0, length) for axis, length in enumerate(drawn.shape)]
    longest = drawn.shape.index(max(drawn.shape))
    next_to = spot[:longest] + [(spot[longest] + 1) % drawn.shape[longest]] + spot[longest + 1:]
    return drawn.at[tuple(spot)].set(smallest).at[tuple(next_to)].set(high)


def setup_inputs(seed: int = 0, part: int = 0) -> dict:
    arg_keys = jax.random.split(jax.random.key(seed), 5)
    part_splits = jax.random.split(jax.random.fold_in(arg_keys[4], part), 5)
    embeddings = draw_embeddings(jax.random.fold_in(jax.random.fold_in(arg_keys[4], part), 71), part)
    bucket_pos = draw_bucket_pos(jax.random.fold_in(jax.random.fold_in(arg_keys[4], part), 71), part)
    tile_valid = draw_tile_valid(jax.random.fold_in(jax.random.fold_in(arg_keys[4], part), 71), part)
    pair_mask = place_ends((jax.random.randint(part_splits[3], (BANDS, N_SHARD), 0, 4) < 3).astype(jnp.int32), jax.random.fold_in(part_splits[3], 1), 0, 1)
    return dict(embeddings=embeddings, bucket_pos=bucket_pos, tile_valid=tile_valid, pair_mask=pair_mask)


beta = 8.0
epsilon = 1e-06

def row_scale(block):
    return lax.rsqrt(lax.optimization_barrier(jnp.mean(jnp.square(block.astype(jnp.float32)), axis=-1)) + epsilon)

def kernel_block(query, query_scale, keys, key_scale):
    gram = jnp.dot(query, keys.T, preferred_element_type=jnp.float32)
    return jnp.exp(beta * (query_scale[:, None] * key_scale[None, :] * gram) / D)

def reference(embeddings, bucket_pos, tile_valid, pair_mask):
    lowered = embeddings.astype(jnp.bfloat16)
    bucketed = jnp.zeros((DOCS, D), jnp.bfloat16).at[bucket_pos].set(lowered)
    bucketed = bucketed.reshape(BANDS, N_SHARD, TILE, D)
    scales = row_scale(bucketed)
    row_index = jnp.arange(TILE, dtype=jnp.int32)
    not_self = (row_index[:, None] != row_index[None, :]).astype(jnp.float32)

    def one_tile(flat):
        band = flat // N_SHARD
        position = flat % N_SHARD

        def tile_at(where):
            valid = (row_index < tile_valid[band, where]).astype(jnp.float32)
            return (bucketed[band, where], scales[band, where], valid)
        own, own_scale, own_valid = tile_at(position)
        lower = jnp.maximum(position - 1, 0)
        upper = jnp.minimum(position + 1, N_SHARD - 1)
        lower_live = ((position >= 1) & (pair_mask[band, lower] == 1)).astype(jnp.float32)
        upper_live = ((position + 1 < N_SHARD) & (pair_mask[band, position] == 1)).astype(jnp.float32)
        numer = jnp.zeros((TILE, D), jnp.float32)
        denom = jnp.zeros((TILE,), jnp.float32)
        for where, gate in ((position, not_self), (lower, lower_live), (upper, upper_live)):
            keys, key_scale, key_valid = tile_at(where)
            kernel = kernel_block(own, own_scale, keys, key_scale) * key_valid[None, :] * gate
            numer = numer + jnp.dot(kernel.astype(jnp.bfloat16), keys, preferred_element_type=jnp.float32)
            denom = denom + lax.optimization_barrier(jnp.sum(kernel, axis=1))
        return jnp.where(own_valid[:, None] > 0, numer / denom[:, None], 0.0)
    result = lax.map(one_tile, jnp.arange(BANDS * N_SHARD, dtype=jnp.int32))
    return result.reshape(BANDS, BAND_ROWS, D)
```

```python
import functools

import jax
import jax.numpy as jnp
from jax import lax
from jax.experimental import pallas as pl
from jax.experimental.pallas import tpu as pltpu
from jax.sharding import PartitionSpec as P

beta = 8.0
epsilon = 1e-06
LOG2E = 1.4426950408889634
MESH = pl.DeviceIdType.MESH
ROWS = 256


def far_first(shards):
    return sorted(range(shards), key=lambda d: -min(d, shards - d))


def dot_t(a, b):
    return lax.dot_general(a, b, (((1,), (1,)), ((), ())), preferred_element_type=jnp.float32)


def kernel(
    shards, subs, cores, cap,
    emb, pos, counts, masks, out,
    low, outgoing, incoming, addr_out, addr_in, acc, own, scale_col, scale_row, near, near_scale,
    denom,
    send, recv, addr_send, addr_recv, near_send, near_recv, ns_send, ns_recv,
):
    tile, width = emb.shape
    bands = subs * cores
    owners = shards * bands
    blocks = tile // ROWS
    slots = bands * cap
    group = lax.axis_index("groups")
    shard = lax.axis_index("shard")
    band = lax.axis_index("sub") * cores + lax.axis_index("cores")
    me = shard * bands + band

    def place(z, b):
        return (group, z, b // cores, b % cores)

    barrier = pltpu.get_barrier_semaphore()

    @pl.loop(1, owners)
    def _(step):
        peer = (me + step) % owners
        pl.semaphore_signal(
            barrier, inc=1, device_id=place(peer // bands, peer % bands), device_id_type=MESH
        )

    low[...] = emb[...].astype(jnp.bfloat16)
    where = pos[...]
    owner = where // tile % shards * bands + where // (shards * tile)
    row = where % tile + 1
    chosen = lax.broadcasted_iota(jnp.int32, (owners, tile), 0) == owner
    upto = lax.broadcasted_iota(jnp.int32, (tile, tile), 0) <= lax.broadcasted_iota(
        jnp.int32, (tile, tile), 1
    )
    rank = jnp.dot(
        jnp.where(chosen, 1.0, 0.0).astype(jnp.bfloat16),
        jnp.where(upto, 1.0, 0.0).astype(jnp.bfloat16),
        preferred_element_type=jnp.float32,
    )
    rank = jnp.sum(jnp.where(chosen, rank, 0.0), axis=0, keepdims=True).astype(jnp.int32) - 1
    slot = owner * cap + rank
    which = lax.broadcasted_iota(jnp.int32, (16, tile), 0)
    parts = jnp.where(which == 0, row // 32, jnp.where(which == 1, row % 32, 0))
    parts = parts.astype(jnp.float32).astype(jnp.bfloat16)

    def data_copy(source, target, z, b):
        return pltpu.make_async_remote_copy(
            src_ref=outgoing.at[target], dst_ref=incoming.at[source],
            send_sem=send.at[target], recv_sem=recv.at[source],
            device_id=place(z, b), device_id_type=MESH,
        )

    def addr_copy(source, target, z, b):
        return pltpu.make_async_remote_copy(
            src_ref=addr_out.at[target], dst_ref=addr_in.at[source],
            send_sem=addr_send.at[target], recv_sem=addr_recv.at[source],
            device_id=place(z, b), device_id_type=MESH,
        )

    order = far_first(shards)
    for step, dz in enumerate(order):
        z = (shard + dz) % shards
        pick = lax.broadcasted_iota(jnp.int32, (slots, tile), 0) + z * slots == slot
        pick = jnp.where(pick, 1.0, 0.0).astype(jnp.bfloat16)
        packed = jnp.dot(pick, low[...], preferred_element_type=jnp.float32)
        outgoing[pl.ds(z * bands, bands)] = packed.astype(jnp.bfloat16).reshape(bands, cap, width)
        address = dot_t(parts, pick)
        address = (32.0 * address[0:1] + address[1:2]).astype(jnp.int32) - 1
        for b in range(bands):
            addr_out[z * bands + b] = address[:, b * cap : (b + 1) * cap]
        if step == 0:
            pl.semaphore_wait(barrier, owners - 1)
        for j in range(1 if dz == 0 else 0, bands):
            b = (band + j) % bands
            addr_copy(me, z * bands + b, z, b).start()
            data_copy(me, z * bands + b, z, b).start()
        if dz == 0:
            incoming[pl.ds(me, 1)] = outgoing[pl.ds(me, 1)]
            addr_in[pl.ds(me, 1)] = addr_out[pl.ds(me, 1)]

    def near_copy(block, side):
        z = (shard + (shards - 1 if side else 1)) % shards
        rows = pl.ds(pl.multiple_of(block * ROWS, ROWS), ROWS)
        return pltpu.make_async_remote_copy(
            src_ref=own.at[rows], dst_ref=near.at[side, rows],
            send_sem=near_send.at[side, block], recv_sem=near_recv.at[side, block],
            device_id=place(z, band), device_id_type=MESH,
        )

    def scale_copy(block, side):
        z = (shard + (shards - 1 if side else 1)) % shards
        return pltpu.make_async_remote_copy(
            src_ref=scale_row.at[block], dst_ref=near_scale.at[side, block],
            send_sem=ns_send.at[side, block], recv_sem=ns_recv.at[side, block],
            device_id=place(z, band), device_id_type=MESH,
        )

    for step, dz in enumerate(order):
        z = (shard + shards - dz) % shards
        for j in range(1 if dz == 0 else 0, bands):
            b = (band + bands - j) % bands
            addr_copy(z * bands + b, z * bands + b, z, b).wait_recv()
            data_copy(z * bands + b, z * bands + b, z, b).wait_recv()
        address = jnp.concatenate([addr_in[z * bands + b] for b in range(bands)], axis=1)

        @pl.loop(0, blocks)
        def _(block):
            rows = pl.ds(pl.multiple_of(block * ROWS, ROWS), ROWS)
            put = lax.broadcasted_iota(jnp.int32, (ROWS, slots), 0) + block * ROWS == address
            put = jnp.where(put, 1.0, 0.0).astype(jnp.bfloat16)
            arrived = incoming[pl.ds(z * bands, bands)].reshape(slots, width)
            total = jnp.dot(put, arrived, preferred_element_type=jnp.float32)
            if step > 0:
                total = total + acc[rows]
            if step < shards - 1:
                acc[rows] = total
            else:
                own[rows] = total.astype(jnp.bfloat16)
                scale = lax.rsqrt(jnp.mean(jnp.square(total), axis=1, keepdims=True) + epsilon)
                scale = jnp.broadcast_to(scale, (ROWS, 128))
                scale_col[rows] = scale
                scale_row[block] = jnp.transpose(scale)[0:1]

                @pl.when(shard < shards - 1)
                def _():
                    scale_copy(block, 0).start()
                    near_copy(block, 0).start()

                @pl.when(shard > 0)
                def _():
                    scale_copy(block, 1).start()
                    near_copy(block, 1).start()

    def add_keys(keys, key_scale, key_weight, first_key, first):
        @pl.loop(0, blocks)
        def _(block):
            rows = pl.ds(pl.multiple_of(block * ROWS, ROWS), ROWS)
            gram = dot_t(own[rows], keys)
            weight = jnp.exp2(
                gram * (scale_col[rows, 0:1] * (beta * LOG2E / width)) * key_scale
            ) * key_weight
            if first_key is not None:
                at = lax.broadcasted_iota(jnp.int32, weight.shape, 0) + block * ROWS
                key = lax.broadcasted_iota(jnp.int32, weight.shape, 1) + first_key
                weight = jnp.where(at == key, 0.0, weight)
            numer = jnp.dot(weight.astype(jnp.bfloat16), keys, preferred_element_type=jnp.float32)
            total = weight[:, 0:128]
            for k in range(128, weight.shape[1], 128):
                total = total + weight[:, k : k + 128]
            if first:
                acc[rows] = numer
                denom[rows] = total
            else:
                acc[rows] += numer
                denom[rows] += total

    lane = lax.broadcasted_iota(jnp.int32, (1, ROWS), 1)

    def counted(block, count):
        return jnp.where(lane + block * ROWS < count, 1.0, 0.0)

    own_count = counts[0, shard]
    for block in range(blocks):
        add_keys(
            own[block * ROWS : (block + 1) * ROWS], scale_row[block], counted(block, own_count),
            block * ROWS, block == 0,
        )

    before, after = (shard + shards - 1) % shards, (shard + 1) % shards
    sides = (
        (shard > 0, counts[0, before], masks[0, before]),
        (shard < shards - 1, counts[0, after], masks[0, shard]),
    )
    for block in range(blocks):
        for side, (there, count, live) in enumerate(sides):

            @pl.when(there)
            def _():
                scale_copy(block, side).wait_recv()
                near_copy(block, side).wait_recv()
                gate = counted(block, jnp.where(live == 1, count, 0))
                add_keys(
                    near[side, block * ROWS : (block + 1) * ROWS], near_scale[side, block], gate,
                    None, False,
                )

    @pl.loop(0, blocks)
    def _(block):
        rows = pl.ds(pl.multiple_of(block * ROWS, ROWS), ROWS)
        total = jnp.sum(denom[rows], axis=1, keepdims=True)
        valid = lax.broadcasted_iota(jnp.int32, (ROWS, 1), 0) + block * ROWS < own_count
        out[rows] = jnp.where(valid, acc[rows] / total, 0.0)

    for dz in order:
        z = (shard + dz) % shards
        for j in range(1 if dz == 0 else 0, bands):
            b = (band + j) % bands
            addr_copy(me, z * bands + b, z, b).wait_send()
            data_copy(me, z * bands + b, z, b).wait_send()
    for side, there in enumerate((shard < shards - 1, shard > 0)):

        @pl.when(there)
        def _():
            for block in range(blocks):
                scale_copy(block, side).wait_send()
                near_copy(block, side).wait_send()


def body(embeddings, bucket_pos, tile_valid, pair_mask):
    shards, subs, cores = (lax.axis_size(a) for a in ("shard", "sub", "cores"))
    owners = shards * subs * cores
    tile, width = embeddings.shape
    cap = 2 * tile // owners
    blocks = tile // ROWS
    vmem = pl.BlockSpec(memory_space=pltpu.VMEM)
    smem = pl.BlockSpec(memory_space=pltpu.SMEM)
    dma = pltpu.SemaphoreType.DMA
    bf16, f32 = jnp.bfloat16, jnp.float32
    result = pl.pallas_call(
        functools.partial(kernel, shards, subs, cores, cap),
        out_shape=jax.ShapeDtypeStruct((tile, width), f32),
        in_specs=[vmem, vmem, smem, smem],
        out_specs=vmem,
        scratch_shapes=[
            pltpu.VMEM((tile, width), bf16),
            pltpu.VMEM((owners, cap, width), bf16),
            pltpu.VMEM((owners, cap, width), bf16),
            pltpu.VMEM((owners, 1, cap), jnp.int32),
            pltpu.VMEM((owners, 1, cap), jnp.int32),
            pltpu.VMEM((tile, width), f32),
            pltpu.VMEM((tile, width), bf16),
            pltpu.VMEM((tile, 128), f32),
            pltpu.VMEM((blocks, 1, ROWS), f32),
            pltpu.VMEM((2, tile, width), bf16),
            pltpu.VMEM((2, blocks, 1, ROWS), f32),
            pltpu.VMEM((tile, 128), f32),
            dma((owners,)), dma((owners,)), dma((owners,)), dma((owners,)),
            dma((2, blocks)), dma((2, blocks)), dma((2, blocks)), dma((2, blocks)),
        ],
        compiler_params=pltpu.CompilerParams(
            collective_id=0, has_side_effects=True, vmem_limit_bytes=48 * 1024 * 1024
        ),
        cost_estimate=pl.CostEstimate(
            flops=20 * tile * tile * width, bytes_accessed=8 * tile * width,
            transcendentals=3 * tile * tile,
        ),
    )(embeddings, bucket_pos.reshape(1, tile), tile_valid, pair_mask)
    return result.reshape(1, tile, width)


def solution(mesh):
    placed = (
        P(("groups", "shard", "sub", "cores"), None),
        P(("groups", "shard", "sub", "cores")),
        P(("groups", "sub", "cores"), None),
        P(("groups", "sub", "cores"), None),
    )
    return jax.shard_map(
        body,
        mesh=mesh,
        in_specs=placed,
        out_specs=P(("groups", "sub", "cores"), "shard", None),
        check_vma=False,
    )
```

```python
import functools

import jax
import jax.numpy as jnp
from jax import lax
from jax.experimental import pallas as pl
from jax.experimental.pallas import tpu as pltpu
from jax.sharding import PartitionSpec as P

beta = 8.0
epsilon = 1e-06
LOG2E = 1.4426950408889634
MESH = pl.DeviceIdType.MESH
KEYS = 512
QUERIES = 256
ROWS = 256


def far_first(shards):
    return sorted(range(shards), key=lambda d: -min(d, shards - d))


def dot_t(a, b):
    return lax.dot_general(a, b, (((1,), (1,)), ((), ())), preferred_element_type=jnp.float32)


def kernel(
    shards, subs, cores, cap,
    emb, pos, counts, masks, out,
    low, outgoing, incoming, addr_out, addr_in, acc, own, scale_col, scale_row, near, near_scale,
    denom,
    send, recv, addr_send, addr_recv, near_send, near_recv, ns_send, ns_recv,
):
    tile, width = emb.shape
    bands = subs * cores
    owners = shards * bands
    blocks = tile // ROWS
    slots = bands * cap
    group = lax.axis_index("groups")
    shard = lax.axis_index("shard")
    band = lax.axis_index("sub") * cores + lax.axis_index("cores")
    me = shard * bands + band

    def place(z, b):
        return (group, z, b // cores, b % cores)

    barrier = pltpu.get_barrier_semaphore()

    @pl.loop(1, owners)
    def _(step):
        peer = (me + step) % owners
        pl.semaphore_signal(
            barrier, inc=1, device_id=place(peer // bands, peer % bands), device_id_type=MESH
        )

    low[...] = emb[...].astype(jnp.bfloat16)
    where = pos[...]
    owner = where // tile % shards * bands + where // (shards * tile)
    row = where % tile + 1
    chosen = lax.broadcasted_iota(jnp.int32, (owners, tile), 0) == owner
    upto = lax.broadcasted_iota(jnp.int32, (tile, tile), 0) <= lax.broadcasted_iota(
        jnp.int32, (tile, tile), 1
    )
    rank = jnp.dot(
        jnp.where(chosen, 1.0, 0.0).astype(jnp.bfloat16),
        jnp.where(upto, 1.0, 0.0).astype(jnp.bfloat16),
        preferred_element_type=jnp.float32,
    )
    rank = jnp.sum(jnp.where(chosen, rank, 0.0), axis=0, keepdims=True).astype(jnp.int32) - 1
    slot = owner * cap + rank
    which = lax.broadcasted_iota(jnp.int32, (16, tile), 0)
    parts = jnp.where(which == 0, row // 32, jnp.where(which == 1, row % 32, 0))
    parts = parts.astype(jnp.float32).astype(jnp.bfloat16)

    def data_copy(source, target, z, b):
        return pltpu.make_async_remote_copy(
            src_ref=outgoing.at[target], dst_ref=incoming.at[source],
            send_sem=send.at[target], recv_sem=recv.at[source],
            device_id=place(z, b), device_id_type=MESH,
        )

    def addr_copy(source, target, z, b):
        return pltpu.make_async_remote_copy(
            src_ref=addr_out.at[target], dst_ref=addr_in.at[source],
            send_sem=addr_send.at[target], recv_sem=addr_recv.at[source],
            device_id=place(z, b), device_id_type=MESH,
        )

    order = far_first(shards)
    for step, dz in enumerate(order):
        z = (shard + dz) % shards
        pick = lax.broadcasted_iota(jnp.int32, (slots, tile), 0) + z * slots == slot
        pick = jnp.where(pick, 1.0, 0.0).astype(jnp.bfloat16)
        packed = jnp.dot(pick, low[...], preferred_element_type=jnp.float32)
        outgoing[pl.ds(z * bands, bands)] = packed.astype(jnp.bfloat16).reshape(bands, cap, width)
        address = dot_t(parts, pick)
        address = (32.0 * address[0:1] + address[1:2]).astype(jnp.int32) - 1
        for b in range(bands):
            addr_out[z * bands + b] = address[:, b * cap : (b + 1) * cap]
        if step == 0:
            pl.semaphore_wait(barrier, owners - 1)
        for j in range(1 if dz == 0 else 0, bands):
            b = (band + j) % bands
            addr_copy(me, z * bands + b, z, b).start()
            data_copy(me, z * bands + b, z, b).start()
        if dz == 0:
            incoming[pl.ds(me, 1)] = outgoing[pl.ds(me, 1)]
            addr_in[pl.ds(me, 1)] = addr_out[pl.ds(me, 1)]

    def near_copy(block, side):
        z = (shard + (shards - 1 if side else 1)) % shards
        rows = pl.ds(pl.multiple_of(block * ROWS, ROWS), ROWS)
        return pltpu.make_async_remote_copy(
            src_ref=own.at[rows], dst_ref=near.at[side, rows],
            send_sem=near_send.at[side, block], recv_sem=near_recv.at[side, block],
            device_id=place(z, band), device_id_type=MESH,
        )

    def scale_copy(block, side):
        z = (shard + (shards - 1 if side else 1)) % shards
        return pltpu.make_async_remote_copy(
            src_ref=scale_row.at[block], dst_ref=near_scale.at[side, block],
            send_sem=ns_send.at[side, block], recv_sem=ns_recv.at[side, block],
            device_id=place(z, band), device_id_type=MESH,
        )

    for step, dz in enumerate(order):
        z = (shard + shards - dz) % shards
        for j in range(1 if dz == 0 else 0, bands):
            b = (band + bands - j) % bands
            addr_copy(z * bands + b, z * bands + b, z, b).wait_recv()
            data_copy(z * bands + b, z * bands + b, z, b).wait_recv()
        address = jnp.concatenate([addr_in[z * bands + b] for b in range(bands)], axis=1)

        for block in range(blocks):
            rows = slice(block * ROWS, (block + 1) * ROWS)
            put = lax.broadcasted_iota(jnp.int32, (ROWS, slots), 0) + block * ROWS == address
            put = jnp.where(put, 1.0, 0.0).astype(jnp.bfloat16)
            arrived = incoming[pl.ds(z * bands, bands)].reshape(slots, width)
            total = jnp.dot(put, arrived, preferred_element_type=jnp.float32)
            if step > 0:
                total = total + acc[rows]
            if step < shards - 1:
                acc[rows] = total
            else:
                own[rows] = total.astype(jnp.bfloat16)
                scale = lax.rsqrt(jnp.mean(jnp.square(total), axis=1, keepdims=True) + epsilon)
                scale = jnp.broadcast_to(scale, (ROWS, 128))
                scale_col[rows] = scale
                scale_row[block] = jnp.transpose(scale)[0:1]

                @pl.when(shard < shards - 1)
                def _():
                    scale_copy(block, 0).start()
                    near_copy(block, 0).start()

                @pl.when(shard > 0)
                def _():
                    scale_copy(block, 1).start()
                    near_copy(block, 1).start()

    def add_keys(keys, key_scale, key_weight, first):
        for start in range(0, tile, QUERIES):
            rows = slice(start, start + QUERIES)
            gram = dot_t(own[rows], keys[...])
            weight = jnp.exp2(
                gram * (scale_col[rows, 0:1] * (beta * LOG2E / width)) * key_scale
            ) * key_weight
            if first:
                at = lax.broadcasted_iota(jnp.int32, weight.shape, 0) + start
                key = lax.broadcasted_iota(jnp.int32, weight.shape, 1)
                weight = jnp.where(at == key, 0.0, weight)
            numer = jnp.dot(
                weight.astype(jnp.bfloat16), keys[...], preferred_element_type=jnp.float32
            )
            total = weight[:, 0:128]
            for k in range(128, weight.shape[1], 128):
                total = total + weight[:, k : k + 128]
            if first:
                acc[rows] = numer
                denom[rows] = total
            else:
                acc[rows] += numer
                denom[rows] += total

    def scales(ref, first, last):
        return jnp.concatenate([ref[block] for block in range(first, last)], axis=1)

    def counted(start, keys, count):
        lane = lax.broadcasted_iota(jnp.int32, (1, keys), 1) + start
        return jnp.where(lane < count, 1.0, 0.0)

    own_count = counts[0, shard]
    add_keys(own, scales(scale_row, 0, blocks), counted(0, tile, own_count), True)

    before, after = (shard + shards - 1) % shards, (shard + 1) % shards
    sides = (
        (shard > 0, counts[0, before], masks[0, before]),
        (shard < shards - 1, counts[0, after], masks[0, shard]),
    )
    for start in range(0, tile, KEYS):
        for side, (there, count, live) in enumerate(sides):

            @pl.when(there)
            def _():
                first, last = start // ROWS, (start + KEYS) // ROWS
                for block in range(first, last):
                    scale_copy(block, side).wait_recv()
                    near_copy(block, side).wait_recv()
                add_keys(
                    near.at[side, start : start + KEYS], scales(near_scale.at[side], first, last),
                    counted(start, KEYS, jnp.where(live == 1, count, 0)), False,
                )

    @pl.loop(0, blocks)
    def _(block):
        rows = pl.ds(pl.multiple_of(block * ROWS, ROWS), ROWS)
        total = jnp.sum(denom[rows], axis=1, keepdims=True)
        valid = lax.broadcasted_iota(jnp.int32, (ROWS, 1), 0) + block * ROWS < own_count
        out[rows] = jnp.where(valid, acc[rows] / total, 0.0)

    for dz in order:
        z = (shard + dz) % shards
        for j in range(1 if dz == 0 else 0, bands):
            b = (band + j) % bands
            addr_copy(me, z * bands + b, z, b).wait_send()
            data_copy(me, z * bands + b, z, b).wait_send()
    for side, there in enumerate((shard < shards - 1, shard > 0)):

        @pl.when(there)
        def _():
            for block in range(blocks):
                scale_copy(block, side).wait_send()
                near_copy(block, side).wait_send()


def body(embeddings, bucket_pos, tile_valid, pair_mask):
    shards, subs, cores = (lax.axis_size(a) for a in ("shard", "sub", "cores"))
    owners = shards * subs * cores
    tile, width = embeddings.shape
    cap = 2 * tile // owners
    blocks = tile // ROWS
    vmem = pl.BlockSpec(memory_space=pltpu.VMEM)
    smem = pl.BlockSpec(memory_space=pltpu.SMEM)
    dma = pltpu.SemaphoreType.DMA
    bf16, f32 = jnp.bfloat16, jnp.float32
    result = pl.pallas_call(
        functools.partial(kernel, shards, subs, cores, cap),
        out_shape=jax.ShapeDtypeStruct((tile, width), f32),
        in_specs=[vmem, vmem, smem, smem],
        out_specs=vmem,
        scratch_shapes=[
            pltpu.VMEM((tile, width), bf16),
            pltpu.VMEM((owners, cap, width), bf16),
            pltpu.VMEM((owners, cap, width), bf16),
            pltpu.VMEM((owners, 1, cap), jnp.int32),
            pltpu.VMEM((owners, 1, cap), jnp.int32),
            pltpu.VMEM((tile, width), f32),
            pltpu.VMEM((tile, width), bf16),
            pltpu.VMEM((tile, 128), f32),
            pltpu.VMEM((blocks, 1, ROWS), f32),
            pltpu.VMEM((2, tile, width), bf16),
            pltpu.VMEM((2, blocks, 1, ROWS), f32),
            pltpu.VMEM((tile, 128), f32),
            dma((owners,)), dma((owners,)), dma((owners,)), dma((owners,)),
            dma((2, blocks)), dma((2, blocks)), dma((2, blocks)), dma((2, blocks)),
        ],
        compiler_params=pltpu.CompilerParams(
            collective_id=0, has_side_effects=True, vmem_limit_bytes=48 * 1024 * 1024
        ),
        cost_estimate=pl.CostEstimate(
            flops=20 * tile * tile * width, bytes_accessed=8 * tile * width,
            transcendentals=3 * tile * tile,
        ),
    )(embeddings, bucket_pos.reshape(1, tile), tile_valid, pair_mask)
    return result.reshape(1, tile, width)


def solution(mesh):
    placed = (
        P(("groups", "shard", "sub", "cores"), None),
        P(("groups", "shard", "sub", "cores")),
        P(("groups", "sub", "cores"), None),
        P(("groups", "sub", "cores"), None),
    )
    return jax.shard_map(
        body,
        mesh=mesh,
        in_specs=placed,
        out_specs=P(("groups", "sub", "cores"), "shard", None),
        check_vma=False,
    )
```

```python
import functools

import jax
import jax.numpy as jnp
from jax import lax
from jax.experimental import pallas as pl
from jax.experimental.pallas import tpu as pltpu
from jax.sharding import PartitionSpec as P

beta = 8.0
epsilon = 1e-06
LOG2E = 1.4426950408889634
MESH = pl.DeviceIdType.MESH
QUERIES = 256
ROWS = 256


def far_first(shards):
    return sorted(range(shards), key=lambda d: -min(d, shards - d))


def dot_t(a, b):
    return lax.dot_general(a, b, (((1,), (1,)), ((), ())), preferred_element_type=jnp.float32)


def kernel(
    shards, subs, cores, cap,
    emb_in, pos_in, counts_in, masks_in, out,
    emb, pos, counts, masks, loads, low, outgoing, incoming, addr_out, addr_in, acc, own, scale_col, scale_row, near, near_scale,
    denom,
    send, recv, addr_send, addr_recv, near_send, near_recv, ns_send, ns_recv,
):
    tile, width = emb_in.shape
    bands = subs * cores
    owners = shards * bands
    blocks = tile // ROWS
    slots = bands * cap
    group = lax.axis_index("groups")
    shard = lax.axis_index("shard")
    band = lax.axis_index("sub") * cores + lax.axis_index("cores")
    me = shard * bands + band

    def place(z, b):
        return (group, z, b // cores, b % cores)

    placing = pltpu.make_async_copy(pos_in, pos, loads.at[0])
    rows_in = pltpu.make_async_copy(emb_in, emb, loads.at[1])
    counting = pltpu.make_async_copy(counts_in, counts, loads.at[2])
    masking = pltpu.make_async_copy(masks_in, masks, loads.at[3])
    for load in (placing, rows_in, counting, masking):
        load.start()

    barrier = pltpu.get_barrier_semaphore()

    @pl.loop(1, owners)
    def _(step):
        peer = (me + step) % owners
        pl.semaphore_signal(
            barrier, inc=1, device_id=place(peer // bands, peer % bands), device_id_type=MESH
        )

    placing.wait()
    where = pos[...]
    owner = where // tile % shards * bands + where // (shards * tile)
    row = where % tile + 1
    chosen = lax.broadcasted_iota(jnp.int32, (owners, tile), 0) == owner
    upto = lax.broadcasted_iota(jnp.int32, (tile, tile), 0) <= lax.broadcasted_iota(
        jnp.int32, (tile, tile), 1
    )
    rank = jnp.dot(
        jnp.where(chosen, 1.0, 0.0).astype(jnp.bfloat16),
        jnp.where(upto, 1.0, 0.0).astype(jnp.bfloat16),
        preferred_element_type=jnp.float32,
    )
    rank = jnp.sum(jnp.where(chosen, rank, 0.0), axis=0, keepdims=True).astype(jnp.int32) - 1
    slot = owner * cap + rank
    which = lax.broadcasted_iota(jnp.int32, (16, tile), 0)
    parts = jnp.where(which == 0, row // 32, jnp.where(which == 1, row % 32, 0))
    parts = parts.astype(jnp.float32).astype(jnp.bfloat16)

    def data_copy(source, target, z, b):
        return pltpu.make_async_remote_copy(
            src_ref=outgoing.at[target], dst_ref=incoming.at[source],
            send_sem=send.at[target], recv_sem=recv.at[source],
            device_id=place(z, b), device_id_type=MESH,
        )

    def addr_copy(source, target, z, b):
        return pltpu.make_async_remote_copy(
            src_ref=addr_out.at[target], dst_ref=addr_in.at[source],
            send_sem=addr_send.at[target], recv_sem=addr_recv.at[source],
            device_id=place(z, b), device_id_type=MESH,
        )

    rows_in.wait()
    low[...] = emb[...].astype(jnp.bfloat16)
    order = far_first(shards)
    for step, dz in enumerate(order):
        z = (shard + dz) % shards
        pick = lax.broadcasted_iota(jnp.int32, (slots, tile), 0) + z * slots == slot
        pick = jnp.where(pick, 1.0, 0.0).astype(jnp.bfloat16)
        packed = jnp.dot(pick, low[...], preferred_element_type=jnp.float32)
        outgoing[pl.ds(z * bands, bands)] = packed.astype(jnp.bfloat16).reshape(bands, cap, width)
        address = dot_t(parts, pick)
        address = (32.0 * address[0:1] + address[1:2]).astype(jnp.int32) - 1
        for b in range(bands):
            addr_out[z * bands + b] = address[:, b * cap : (b + 1) * cap]
        if step == 0:
            pl.semaphore_wait(barrier, owners - 1)
        for j in range(1 if dz == 0 else 0, bands):
            b = (band + j) % bands
            addr_copy(me, z * bands + b, z, b).start()
            data_copy(me, z * bands + b, z, b).start()
        if dz == 0:
            incoming[pl.ds(me, 1)] = outgoing[pl.ds(me, 1)]
            addr_in[pl.ds(me, 1)] = addr_out[pl.ds(me, 1)]

    def near_copy(block, side):
        z = (shard + (shards - 1 if side else 1)) % shards
        rows = pl.ds(pl.multiple_of(block * ROWS, ROWS), ROWS)
        return pltpu.make_async_remote_copy(
            src_ref=own.at[rows], dst_ref=near.at[side, rows],
            send_sem=near_send.at[side, block], recv_sem=near_recv.at[side, block],
            device_id=place(z, band), device_id_type=MESH,
        )

    def scale_copy(block, side):
        z = (shard + (shards - 1 if side else 1)) % shards
        return pltpu.make_async_remote_copy(
            src_ref=scale_row.at[block], dst_ref=near_scale.at[side, block],
            send_sem=ns_send.at[side, block], recv_sem=ns_recv.at[side, block],
            device_id=place(z, band), device_id_type=MESH,
        )

    for step, dz in enumerate([0] + [d for d in order if d != 0]):
        z = (shard + shards - dz) % shards
        for j in range(1 if dz == 0 else 0, bands):
            b = (band + bands - j) % bands
            addr_copy(z * bands + b, z * bands + b, z, b).wait_recv()
            data_copy(z * bands + b, z * bands + b, z, b).wait_recv()
        address = jnp.concatenate([addr_in[z * bands + b] for b in range(bands)], axis=1)

        for block in range(blocks):
            rows = slice(block * ROWS, (block + 1) * ROWS)
            put = lax.broadcasted_iota(jnp.int32, (ROWS, slots), 0) + block * ROWS == address
            put = jnp.where(put, 1.0, 0.0).astype(jnp.bfloat16)
            arrived = incoming[pl.ds(z * bands, bands)].reshape(slots, width)
            total = jnp.dot(put, arrived, preferred_element_type=jnp.float32)
            if step > 0:
                total = total + acc[rows]
            if step < shards - 1:
                acc[rows] = total
            else:
                own[rows] = total.astype(jnp.bfloat16)
                scale = lax.rsqrt(jnp.mean(jnp.square(total), axis=1, keepdims=True) + epsilon)
                scale = jnp.broadcast_to(scale, (ROWS, 128))
                scale_col[rows] = scale
                scale_row[block] = jnp.transpose(scale)[0:1]

                @pl.when(shard < shards - 1)
                def _():
                    scale_copy(block, 0).start()
                    near_copy(block, 0).start()

                @pl.when(shard > 0)
                def _():
                    scale_copy(block, 1).start()
                    near_copy(block, 1).start()

    def add_keys(keys, key_scale, key_weight, first):
        for start in range(0, tile, QUERIES):
            rows = slice(start, start + QUERIES)
            gram = dot_t(own[rows], keys[...])
            weight = jnp.exp2(
                gram * (scale_col[rows, 0:1] * (beta * LOG2E / width)) * key_scale
            ) * key_weight
            if first:
                at = lax.broadcasted_iota(jnp.int32, weight.shape, 0) + start
                key = lax.broadcasted_iota(jnp.int32, weight.shape, 1)
                weight = jnp.where(at == key, 0.0, weight)
            numer = jnp.dot(
                weight.astype(jnp.bfloat16), keys[...], preferred_element_type=jnp.float32
            )
            total = weight[:, 0:128]
            for k in range(128, weight.shape[1], 128):
                total = total + weight[:, k : k + 128]
            if first:
                acc[rows] = numer
                denom[rows] = total
            else:
                acc[rows] += numer
                denom[rows] += total

    def scales(ref, first, last):
        return jnp.concatenate([ref[block] for block in range(first, last)], axis=1)

    def counted(start, keys, count):
        lane = lax.broadcasted_iota(jnp.int32, (1, keys), 1) + start
        return jnp.where(lane < count, 1.0, 0.0)

    counting.wait()
    masking.wait()
    own_count = counts[0, shard]
    add_keys(own, scales(scale_row, 0, blocks), counted(0, tile, own_count), True)

    before, after = (shard + shards - 1) % shards, (shard + 1) % shards
    sides = (
        (shard > 0, counts[0, before], masks[0, before]),
        (shard < shards - 1, counts[0, after], masks[0, shard]),
    )
    half = tile // 2
    pieces = [(0, half)] + [(start, ROWS) for start in range(half, tile, ROWS)]
    for start, size in pieces:
        for side, (there, count, live) in enumerate(sides):

            @pl.when(there)
            def _():
                first, last = start // ROWS, (start + size) // ROWS
                for block in range(first, last):
                    scale_copy(block, side).wait_recv()
                    near_copy(block, side).wait_recv()
                add_keys(
                    near.at[side, start : start + size], scales(near_scale.at[side], first, last),
                    counted(start, size, jnp.where(live == 1, count, 0)), False,
                )

    for block in range(blocks):
        rows = slice(block * ROWS, (block + 1) * ROWS)
        total = jnp.sum(denom[rows], axis=1, keepdims=True)
        valid = lax.broadcasted_iota(jnp.int32, (ROWS, 1), 0) + block * ROWS < own_count
        out[rows] = jnp.where(valid, acc[rows] / total, 0.0)

    for dz in order:
        z = (shard + dz) % shards
        for j in range(1 if dz == 0 else 0, bands):
            b = (band + j) % bands
            addr_copy(me, z * bands + b, z, b).wait_send()
            data_copy(me, z * bands + b, z, b).wait_send()
    for side, there in enumerate((shard < shards - 1, shard > 0)):

        @pl.when(there)
        def _():
            for block in range(blocks):
                scale_copy(block, side).wait_send()
                near_copy(block, side).wait_send()


def body(embeddings, bucket_pos, tile_valid, pair_mask):
    shards, subs, cores = (lax.axis_size(a) for a in ("shard", "sub", "cores"))
    owners = shards * subs * cores
    tile, width = embeddings.shape
    cap = 2 * tile // owners
    blocks = tile // ROWS
    vmem = pl.BlockSpec(memory_space=pltpu.VMEM)
    hbm = pl.BlockSpec(memory_space=pltpu.HBM)
    dma = pltpu.SemaphoreType.DMA
    bf16, f32 = jnp.bfloat16, jnp.float32
    result = pl.pallas_call(
        functools.partial(kernel, shards, subs, cores, cap),
        out_shape=jax.ShapeDtypeStruct((tile, width), f32),
        in_specs=[hbm, hbm, hbm, hbm],
        out_specs=vmem,
        scratch_shapes=[
            pltpu.VMEM((tile, width), f32),
            pltpu.VMEM((1, tile), jnp.int32),
            pltpu.SMEM(tile_valid.shape, jnp.int32),
            pltpu.SMEM(pair_mask.shape, jnp.int32),
            dma((4,)),
            pltpu.VMEM((tile, width), bf16),
            pltpu.VMEM((owners, cap, width), bf16),
            pltpu.VMEM((owners, cap, width), bf16),
            pltpu.VMEM((owners, 1, cap), jnp.int32),
            pltpu.VMEM((owners, 1, cap), jnp.int32),
            pltpu.VMEM((tile, width), f32),
            pltpu.VMEM((tile, width), bf16),
            pltpu.VMEM((tile, 128), f32),
            pltpu.VMEM((blocks, 1, ROWS), f32),
            pltpu.VMEM((2, tile, width), bf16),
            pltpu.VMEM((2, blocks, 1, ROWS), f32),
            pltpu.VMEM((tile, 128), f32),
            dma((owners,)), dma((owners,)), dma((owners,)), dma((owners,)),
            dma((2, blocks)), dma((2, blocks)), dma((2, blocks)), dma((2, blocks)),
        ],
        compiler_params=pltpu.CompilerParams(
            collective_id=0, has_side_effects=True, vmem_limit_bytes=48 * 1024 * 1024
        ),
        cost_estimate=pl.CostEstimate(
            flops=20 * tile * tile * width, bytes_accessed=8 * tile * width,
            transcendentals=3 * tile * tile,
        ),
    )(embeddings, bucket_pos.reshape(1, tile), tile_valid, pair_mask)
    return result.reshape(1, tile, width)


def solution(mesh):
    placed = (
        P(("groups", "shard", "sub", "cores"), None),
        P(("groups", "shard", "sub", "cores")),
        P(("groups", "sub", "cores"), None),
        P(("groups", "sub", "cores"), None),
    )
    return jax.shard_map(
        body,
        mesh=mesh,
        in_specs=placed,
        out_specs=P(("groups", "sub", "cores"), "shard", None),
        check_vma=False,
    )
```

```python
import functools

import jax
import jax.numpy as jnp
from jax import lax
from jax.experimental import pallas as pl
from jax.experimental.pallas import tpu as pltpu
from jax.sharding import PartitionSpec as P

beta = 8.0
epsilon = 1e-06
LOG2E = 1.4426950408889634
MESH = pl.DeviceIdType.MESH
QUERIES = 256
ROWS = 256


def far_first(shards):
    return sorted(range(shards), key=lambda d: -min(d, shards - d))


def dot_t(a, b):
    return lax.dot_general(a, b, (((1,), (1,)), ((), ())), preferred_element_type=jnp.float32)


def kernel(
    shards, subs, cores, cap,
    emb_in, pos_in, counts_in, masks_in, out,
    emb, pos, counts, masks, loads, low, outgoing, incoming, addr_out, addr_in, acc, own, scale_col, scale_row, near, near_scale,
    denom,
    send, recv, addr_send, addr_recv, near_send, near_recv, ns_send, ns_recv,
):
    tile, width = emb_in.shape
    bands = subs * cores
    owners = shards * bands
    blocks = tile // ROWS
    slots = bands * cap
    group = lax.axis_index("groups")
    shard = lax.axis_index("shard")
    band = lax.axis_index("sub") * cores + lax.axis_index("cores")
    me = shard * bands + band

    def place(z, b):
        return (group, z, b // cores, b % cores)

    placing = pltpu.make_async_copy(pos_in, pos, loads.at[0])
    rows_in = pltpu.make_async_copy(emb_in, emb, loads.at[1])
    counting = pltpu.make_async_copy(counts_in, counts, loads.at[2])
    masking = pltpu.make_async_copy(masks_in, masks, loads.at[3])
    for load in (placing, rows_in, counting, masking):
        load.start()

    barrier = pltpu.get_barrier_semaphore()

    @pl.loop(1, owners)
    def _(step):
        peer = (me + step) % owners
        pl.semaphore_signal(
            barrier, inc=1, device_id=place(peer // bands, peer % bands), device_id_type=MESH
        )

    placing.wait()
    where = pos[...]
    owner = where // tile % shards * bands + where // (shards * tile)
    row = where % tile + 1
    chosen = lax.broadcasted_iota(jnp.int32, (owners, tile), 0) == owner
    upto = lax.broadcasted_iota(jnp.int32, (128, 128), 0) <= lax.broadcasted_iota(
        jnp.int32, (128, 128), 1
    )
    ones = jnp.where(chosen, 1.0, 0.0)
    runs = jnp.dot(
        jnp.concatenate([ones[:, k : k + 128] for k in range(0, tile, 128)], axis=0).astype(
            jnp.bfloat16
        ),
        jnp.where(upto, 1.0, 0.0).astype(jnp.bfloat16),
        preferred_element_type=jnp.float32,
    )
    before_run = jnp.zeros((owners, 1), jnp.float32)
    ranks = []
    for k in range(tile // 128):
        run = runs[k * owners : (k + 1) * owners]
        ranks.append(run + before_run)
        before_run = before_run + run[:, 127:128]
    rank = jnp.concatenate(ranks, axis=1)
    rank = jnp.sum(jnp.where(chosen, rank, 0.0), axis=0, keepdims=True).astype(jnp.int32) - 1
    slot = owner * cap + rank
    which = lax.broadcasted_iota(jnp.int32, (16, tile), 0)
    parts = jnp.where(which == 0, row // 32, jnp.where(which == 1, row % 32, 0))
    parts = parts.astype(jnp.float32).astype(jnp.bfloat16)

    def data_copy(source, target, z, b):
        return pltpu.make_async_remote_copy(
            src_ref=outgoing.at[target], dst_ref=incoming.at[source],
            send_sem=send.at[target], recv_sem=recv.at[source],
            device_id=place(z, b), device_id_type=MESH,
        )

    def addr_copy(source, target, z, b):
        return pltpu.make_async_remote_copy(
            src_ref=addr_out.at[target], dst_ref=addr_in.at[source],
            send_sem=addr_send.at[target], recv_sem=addr_recv.at[source],
            device_id=place(z, b), device_id_type=MESH,
        )

    rows_in.wait()
    low[...] = emb[...].astype(jnp.bfloat16)
    order = far_first(shards)
    for step, dz in enumerate(order):
        z = (shard + dz) % shards
        pick = lax.broadcasted_iota(jnp.int32, (slots, tile), 0) + z * slots == slot
        pick = jnp.where(pick, 1.0, 0.0).astype(jnp.bfloat16)
        packed = jnp.dot(pick, low[...], preferred_element_type=jnp.float32)
        outgoing[pl.ds(z * bands, bands)] = packed.astype(jnp.bfloat16).reshape(bands, cap, width)
        address = dot_t(parts, pick)
        address = (32.0 * address[0:1] + address[1:2]).astype(jnp.int32) - 1
        for b in range(bands):
            addr_out[z * bands + b] = address[:, b * cap : (b + 1) * cap]
        if step == 0:
            pl.semaphore_wait(barrier, owners - 1)
        for j in range(1 if dz == 0 else 0, bands):
            b = (band + j) % bands
            addr_copy(me, z * bands + b, z, b).start()
            data_copy(me, z * bands + b, z, b).start()
        if dz == 0:
            incoming[pl.ds(me, 1)] = outgoing[pl.ds(me, 1)]
            addr_in[pl.ds(me, 1)] = addr_out[pl.ds(me, 1)]

    def near_copy(block, side):
        z = (shard + (shards - 1 if side else 1)) % shards
        rows = pl.ds(pl.multiple_of(block * ROWS, ROWS), ROWS)
        return pltpu.make_async_remote_copy(
            src_ref=own.at[rows], dst_ref=near.at[side, rows],
            send_sem=near_send.at[side, block], recv_sem=near_recv.at[side, block],
            device_id=place(z, band), device_id_type=MESH,
        )

    def scale_copy(block, side):
        z = (shard + (shards - 1 if side else 1)) % shards
        return pltpu.make_async_remote_copy(
            src_ref=scale_row.at[block], dst_ref=near_scale.at[side, block],
            send_sem=ns_send.at[side, block], recv_sem=ns_recv.at[side, block],
            device_id=place(z, band), device_id_type=MESH,
        )

    for step, dz in enumerate([0] + [d for d in order if d != 0]):
        z = (shard + shards - dz) % shards
        for j in range(1 if dz == 0 else 0, bands):
            b = (band + bands - j) % bands
            addr_copy(z * bands + b, z * bands + b, z, b).wait_recv()
            data_copy(z * bands + b, z * bands + b, z, b).wait_recv()
        address = jnp.concatenate([addr_in[z * bands + b] for b in range(bands)], axis=1)

        for block in range(blocks):
            rows = slice(block * ROWS, (block + 1) * ROWS)
            put = lax.broadcasted_iota(jnp.int32, (ROWS, slots), 0) + block * ROWS == address
            put = jnp.where(put, 1.0, 0.0).astype(jnp.bfloat16)
            arrived = incoming[pl.ds(z * bands, bands)].reshape(slots, width)
            total = jnp.dot(put, arrived, preferred_element_type=jnp.float32)
            if step > 0:
                total = total + acc[rows]
            if step < shards - 1:
                acc[rows] = total
            else:
                own[rows] = total.astype(jnp.bfloat16)
                scale = lax.rsqrt(jnp.mean(jnp.square(total), axis=1, keepdims=True) + epsilon)
                scale = jnp.broadcast_to(scale, (ROWS, 128))
                scale_col[rows] = scale
                scale_row[block] = jnp.transpose(scale)[0:1]

                @pl.when(shard < shards - 1)
                def _():
                    scale_copy(block, 0).start()
                    near_copy(block, 0).start()

                @pl.when(shard > 0)
                def _():
                    scale_copy(block, 1).start()
                    near_copy(block, 1).start()

    def add_keys(keys, key_scale, key_weight, first):
        for start in range(0, tile, QUERIES):
            rows = slice(start, start + QUERIES)
            gram = dot_t(own[rows], keys[...])
            weight = jnp.exp2(
                gram * (scale_col[rows, 0:1] * (beta * LOG2E / width)) * key_scale
            ) * key_weight
            if first:
                at = lax.broadcasted_iota(jnp.int32, weight.shape, 0) + start
                key = lax.broadcasted_iota(jnp.int32, weight.shape, 1)
                weight = jnp.where(at == key, 0.0, weight)
            numer = jnp.dot(
                weight.astype(jnp.bfloat16), keys[...], preferred_element_type=jnp.float32
            )
            total = weight[:, 0:128]
            for k in range(128, weight.shape[1], 128):
                total = total + weight[:, k : k + 128]
            if first:
                acc[rows] = numer
                denom[rows] = total
            else:
                acc[rows] += numer
                denom[rows] += total

    def scales(ref, first, last):
        return jnp.concatenate([ref[block] for block in range(first, last)], axis=1)

    def counted(start, keys, count):
        lane = lax.broadcasted_iota(jnp.int32, (1, keys), 1) + start
        return jnp.where(lane < count, 1.0, 0.0)

    counting.wait()
    masking.wait()
    own_count = counts[0, shard]
    add_keys(own, scales(scale_row, 0, blocks), counted(0, tile, own_count), True)

    before, after = (shard + shards - 1) % shards, (shard + 1) % shards
    sides = (
        (shard > 0, counts[0, before], masks[0, before]),
        (shard < shards - 1, counts[0, after], masks[0, shard]),
    )
    half = tile // 2
    pieces = [(0, half)] + [(start, ROWS) for start in range(half, tile, ROWS)]
    for start, size in pieces:
        for side, (there, count, live) in enumerate(sides):

            @pl.when(there)
            def _():
                first, last = start // ROWS, (start + size) // ROWS
                for block in range(first, last):
                    scale_copy(block, side).wait_recv()
                    near_copy(block, side).wait_recv()
                add_keys(
                    near.at[side, start : start + size], scales(near_scale.at[side], first, last),
                    counted(start, size, jnp.where(live == 1, count, 0)), False,
                )

    for block in range(blocks):
        rows = slice(block * ROWS, (block + 1) * ROWS)
        total = jnp.sum(denom[rows], axis=1, keepdims=True)
        valid = lax.broadcasted_iota(jnp.int32, (ROWS, 1), 0) + block * ROWS < own_count
        out[rows] = jnp.where(valid, acc[rows] / total, 0.0)

    for dz in order:
        z = (shard + dz) % shards
        for j in range(1 if dz == 0 else 0, bands):
            b = (band + j) % bands
            addr_copy(me, z * bands + b, z, b).wait_send()
            data_copy(me, z * bands + b, z, b).wait_send()
    for side, there in enumerate((shard < shards - 1, shard > 0)):

        @pl.when(there)
        def _():
            for block in range(blocks):
                scale_copy(block, side).wait_send()
                near_copy(block, side).wait_send()


def body(embeddings, bucket_pos, tile_valid, pair_mask):
    shards, subs, cores = (lax.axis_size(a) for a in ("shard", "sub", "cores"))
    owners = shards * subs * cores
    tile, width = embeddings.shape
    cap = 2 * tile // owners
    blocks = tile // ROWS
    vmem = pl.BlockSpec(memory_space=pltpu.VMEM)
    hbm = pl.BlockSpec(memory_space=pltpu.HBM)
    dma = pltpu.SemaphoreType.DMA
    bf16, f32 = jnp.bfloat16, jnp.float32
    result = pl.pallas_call(
        functools.partial(kernel, shards, subs, cores, cap),
        out_shape=jax.ShapeDtypeStruct((tile, width), f32),
        in_specs=[hbm, hbm, hbm, hbm],
        out_specs=vmem,
        scratch_shapes=[
            pltpu.VMEM((tile, width), f32),
            pltpu.VMEM((1, tile), jnp.int32),
            pltpu.SMEM(tile_valid.shape, jnp.int32),
            pltpu.SMEM(pair_mask.shape, jnp.int32),
            dma((4,)),
            pltpu.VMEM((tile, width), bf16),
            pltpu.VMEM((owners, cap, width), bf16),
            pltpu.VMEM((owners, cap, width), bf16),
            pltpu.VMEM((owners, 1, cap), jnp.int32),
            pltpu.VMEM((owners, 1, cap), jnp.int32),
            pltpu.VMEM((tile, width), f32),
            pltpu.VMEM((tile, width), bf16),
            pltpu.VMEM((tile, 128), f32),
            pltpu.VMEM((blocks, 1, ROWS), f32),
            pltpu.VMEM((2, tile, width), bf16),
            pltpu.VMEM((2, blocks, 1, ROWS), f32),
            pltpu.VMEM((tile, 128), f32),
            dma((owners,)), dma((owners,)), dma((owners,)), dma((owners,)),
            dma((2, blocks)), dma((2, blocks)), dma((2, blocks)), dma((2, blocks)),
        ],
        compiler_params=pltpu.CompilerParams(
            collective_id=0, has_side_effects=True, vmem_limit_bytes=48 * 1024 * 1024
        ),
        cost_estimate=pl.CostEstimate(
            flops=20 * tile * tile * width, bytes_accessed=8 * tile * width,
            transcendentals=3 * tile * tile,
        ),
    )(embeddings, bucket_pos.reshape(1, tile), tile_valid, pair_mask)
    return result.reshape(1, tile, width)


def solution(mesh):
    placed = (
        P(("groups", "shard", "sub", "cores"), None),
        P(("groups", "shard", "sub", "cores")),
        P(("groups", "sub", "cores"), None),
        P(("groups", "sub", "cores"), None),
    )
    return jax.shard_map(
        body,
        mesh=mesh,
        in_specs=placed,
        out_specs=P(("groups", "sub", "cores"), "shard", None),
        check_vma=False,
    )
```
